32 devices in a mesh: grp: 8 (over y, x, core), intra: 4 (over z).
Axes of the slice: x: 2, y: 2, z: 4, core: 2. Of those that a mesh axis runs over, the one named last changes fastest.
Arguments:
- activations: bfloat16 [576, 4096], P('intra'), may hold values from -6 to 6
- cotangent: bfloat16 [576, 11520], P('intra', 'grp'), may hold values from -6 to 6
- weight_quant: bfloat16 [11520, 4096], P('grp', 'intra'), may hold values from -1 to 1
- weight_scale: bfloat16 [1440, 16], P('grp', 'intra'), may hold values from 0.0049743652 to 0.049804688
Outputs:
- input_grad: bfloat16 [576, 4096], P('intra')
- grad_quant: bfloat16 [11520, 4096], P('grp', 'intra')
- grad_scale: float32 [1440, 16], P('grp', 'intra')
The draws below stay inside these ranges and needn't reach their ends.
All inputs are finite; a program needn't handle non-finite values.
Results may differ from the reference program's by a relative error of at most 0.0053.
Values may be sent and summed in bfloat16 or wider, within the bound.
A program may use at most 192 MiB of HBM per device.

```python
import math
import jax
import jax.numpy as jnp
from jax import lax

D = 4096
FW = 11520
QROWS = 8
QCOLS = 256
TOK_DEV = 144
TOKENS = 576
N_INTRA = 4


def levels(key, dims, split, least, high):
    loudness, own = 1.0, jax.random.fold_in(key, 6)
    for axis_at, parts in split:
        heights = jnp.exp(jax.random.uniform(jax.random.fold_in(own, axis_at), (parts,), jnp.float32, least / len(split), high / len(split)))
        loudness = loudness * jnp.repeat(heights, dims[axis_at] // parts).reshape([-1 if axis == axis_at else 1 for axis in range(len(dims))])
    return loudness


def noise(stream_key, extent, spread, reach, split=(), kind=jnp.bfloat16):
    entries = jax.random.normal(stream_key, extent, jnp.float32) * spread
    if len(split) > 0:
        entries = levels(stream_key, extent, split, -0.22, 0.18) * entries
    return jnp.clip(entries, min=-reach, max=reach).astype(kind)


def setup_inputs(seed: int = 0) -> dict:
    key_of = jax.random.split(jax.random.key(seed), 5)
    return {
        "activations": noise(key_of[0], (TOKENS, D), 1.0, 6.0, ((0, 4),)),
        "cotangent": noise(key_of[1], (TOKENS, FW), 1.0, 6.0, ((0, 4), (1, 8))),
        "weight_quant": jnp.clip(jax.random.uniform(key_of[2], (FW, D), jnp.float32, -1.0, 1.0) * levels(key_of[2], (FW, D), ((0, 8), (1, 4)), -0.4, 0.0), -1.0, 1.0).astype(jnp.bfloat16),
        "weight_scale": jnp.clip(jnp.exp(math.log(0.049804688) - 2.3038113 * jax.random.uniform(key_of[3], (FW // QROWS, D // QCOLS), jnp.float32) ** levels(key_of[3], (FW // QROWS, D // QCOLS), ((0, 8), (1, 4)), -0.2, 0.2)), 0.0049743652, 0.049804688).astype(jnp.bfloat16),
    }


epsilon = 1e-6


def block_view(values):
    row_count, col_count = values.shape
    return values.reshape(row_count // QROWS, QROWS, col_count // QCOLS, QCOLS)


def apply_scale(values, scales):
    return (block_view(values) * scales[:, None, :, None]).reshape(values.shape)


def divide_scale(values, scales):
    return (block_view(values) / scales[:, None, :, None]).reshape(values.shape)


def block_peak(values):
    return jnp.max(jnp.abs(block_view(values)), axis=(1, 3)) + epsilon


def reference(activations, cotangent, weight_quant, weight_scale):
    weight = apply_scale(weight_quant.astype(jnp.float32), weight_scale.astype(jnp.float32)).astype(jnp.bfloat16)
    input_grad = jnp.dot(cotangent, weight, preferred_element_type=jnp.float32).astype(jnp.bfloat16)
    act_blocks = activations.reshape(N_INTRA, TOK_DEV, D)
    cot_blocks = cotangent.reshape(N_INTRA, TOK_DEV, FW)

    def accumulate(summed, inputs):
        act_block, cot_block = inputs
        partial_value = (jnp.dot(cot_block.T, act_block, preferred_element_type=jnp.float32) / TOKENS).astype(jnp.bfloat16)
        partial_value = lax.optimization_barrier(partial_value)
        return summed + partial_value.astype(jnp.float32), None

    summed, _ = lax.scan(accumulate, jnp.zeros((FW, D), jnp.float32), (act_blocks, cot_blocks))
    grad_scale = block_peak(summed)
    grad_quant = divide_scale(summed, grad_scale).astype(jnp.bfloat16)
    return input_grad, grad_quant, grad_scale
```

```python
import functools

import jax
import jax.numpy as jnp
from jax import lax
from jax.experimental import pallas as pl
from jax.experimental.pallas import tpu as pltpu
from jax.sharding import PartitionSpec as P

QROWS = 8
QCOLS = 256
MESH = pl.DeviceIdType.MESH

epsilon = 1e-06


def dequantize(quantized, scales):
    row_count, col_count = quantized.shape
    blocks = quantized.astype(jnp.float32).reshape(
        row_count // QROWS, QROWS, col_count // QCOLS, QCOLS
    )
    return (blocks * scales.astype(jnp.float32)[:, None, :, None]).reshape(row_count, col_count)


def summed_rows(source, weight):
    shares = lax.psum_scatter(
        jnp.dot(source, weight, preferred_element_type=jnp.float32),
        "grp",
        scatter_dimension=0,
        tiled=True,
    )
    return lax.all_gather(shares.astype(jnp.bfloat16), "grp", axis=0, tiled=True)


def requantize(summed):
    block_count, _, local_cols = summed.shape
    blocks = summed.reshape(block_count, QROWS, local_cols // QCOLS, QCOLS)
    peak_value = jnp.max(jnp.abs(blocks), axis=(1, 3)) + epsilon
    requant = (blocks / peak_value[:, None, :, None]).astype(jnp.bfloat16)
    return (requant.reshape(block_count, QROWS, local_cols), peak_value)


def general(activations, cotangent, weight_quant, weight_scale):
    intra_count = lax.axis_size("intra")
    quant_all, scale_all = (
        lax.all_gather(weight_quant, "intra", axis=1, tiled=True),
        lax.all_gather(weight_scale, "intra", axis=1, tiled=True),
    )
    weight = dequantize(quant_all, scale_all).astype(jnp.bfloat16)
    total_tokens = activations.shape[0] * intra_count
    tok_rows = activations.shape[0]
    hidden_rows = cotangent.shape[1]
    act_cols = lax.all_to_all(activations, "intra", split_axis=1, concat_axis=0, tiled=True)
    cot_all = lax.all_gather(cotangent, "intra", axis=0, tiled=True)
    input_grad = summed_rows(cotangent, weight)
    local_cols = act_cols.shape[1]
    act_split = act_cols.reshape(intra_count, tok_rows, local_cols)
    cot_split = cot_all.reshape(intra_count, tok_rows, hidden_rows)
    partials = (
        jnp.einsum("bth,btc->bhc", cot_split, act_split, preferred_element_type=jnp.float32)
        / total_tokens
    )
    partials = lax.optimization_barrier(partials.astype(jnp.bfloat16))
    summed = jnp.sum(partials.astype(jnp.float32), axis=0)
    grad_quant, grad_scale = requantize(summed.reshape(hidden_rows // QROWS, QROWS, local_cols))
    grad_quant = grad_quant.reshape(hidden_rows, local_cols)
    return (input_grad, grad_quant, grad_scale)


def kernel(
    n, act, cot, wq, wscale, out, gq, gscale,
    cot_all, act_all, wq_v, w, psend, red, fin, gq_v,
    local_sem, cot_send, cot_recv, aa_send, aa_recv, ab_send, ab_recv, ac_send, ac_recv,
    red_send, red_recv, fin_send, fin_recv, ob_send, ob_recv, oc_send, oc_recv, gq_sem,
):
    g, z = lax.axis_index("grp"), lax.axis_index("intra")
    chip, core = g // 2, g % 2
    q = core * 4 + chip
    toks = cot.shape[0]
    hidden, cols = wq.shape
    width = cols // 8
    partner = chip * 2 + (1 - core)

    def at_piece(plane, piece, count=1):
        return pl.ds(pl.multiple_of(plane * cols + piece * width, width), count * width)

    def chip_at(k):
        return ((chip + k) % 4) * 2 + core

    def plane_at(r):
        return (z + r) % n

    def remote(src, dst, send, recv, to_g, to_z):
        return pltpu.make_async_remote_copy(
            src_ref=src, dst_ref=dst, send_sem=send, recv_sem=recv,
            device_id=(to_g, to_z), device_id_type=MESH,
        )

    load_wq = pltpu.make_async_copy(wq, wq_v, local_sem.at[0])
    load_cot = pltpu.make_async_copy(cot, cot_all.at[0], local_sem.at[1])
    load_act = pltpu.make_async_copy(
        act.at[:, pl.ds(pl.multiple_of(z * cols, width), cols)], act_all.at[0], local_sem.at[2]
    )
    load_cot.start()
    load_wq.start()
    load_act.start()

    barrier = pltpu.get_barrier_semaphore()
    for k in range(1, 8):
        t = (q + k) % 8
        pl.semaphore_signal(barrier, inc=1, device_id=((t % 4) * 2 + t // 4, z), device_id_type=MESH)
    for r in range(1, n):
        pl.semaphore_signal(barrier, inc=1, device_id=(g, plane_at(r)), device_id_type=MESH)
    pl.semaphore_wait(barrier, 7 + n - 1)

    own_right = remote(cot, cot_all.at[n - 1], cot_send.at[n], cot_recv.at[n - 1], g, jnp.minimum(z + 1, n - 1))
    own_left = remote(cot, cot_all.at[1], cot_send.at[0], cot_recv.at[1], g, jnp.maximum(z - 1, 0))

    @pl.when(z < n - 1)
    def _():
        own_right.start()

    @pl.when(z > 0)
    def _():
        own_left.start()

    def act_z(r):
        to = plane_at(r)
        return remote(
            act.at[:, at_piece(to, q)], act_all.at[n - r, :, at_piece(0, q)],
            aa_send.at[r], aa_recv.at[n - r], g, to,
        )

    for r in range(1, n):
        act_z(r).start()

    def act_plane(k):
        piece = act_all.at[pl.ds(1, n - 1), :, at_piece(0, q)]
        return remote(piece, piece, ab_send.at[k], ab_recv.at[k], chip_at(k), z)

    def act_core():
        half = act_all.at[pl.ds(1, n - 1), :, at_piece(0, core * 4, 4)]
        return remote(half, half, ac_send, ac_recv, partner, z)

    load_wq.wait()
    step = 2 * QROWS * 9 if hidden % (2 * QROWS * 9) == 0 else hidden

    @pl.loop(0, hidden // step)
    def _(i):
        rows = pl.ds(pl.multiple_of(i * step, step), step)
        scale = wscale[rows, :].astype(jnp.float32)
        for j in range(cols // QCOLS):
            at = pl.ds(j * QCOLS, QCOLS)
            w[rows, at] = (wq_v[rows, at].astype(jnp.float32) * scale[:, j : j + 1]).astype(w.dtype)

    def red_copy(r, k):
        t = (q + k) % 8
        return remote(
            psend.at[r, :, at_piece(0, t)], red.at[r, q],
            red_send.at[r, k], red_recv.at[r, k], (t % 4) * 2 + t // 4, z,
        )

    def partial(r):
        psend[r] = jnp.dot(cot_all[r], w[...], preferred_element_type=jnp.float32).astype(psend.dtype)
        for k in range(1, 8):
            red_copy(r, k).start()

    def piece_sum(r):
        total = psend[r, :, at_piece(0, q)].astype(jnp.float32)
        for k in range(1, 8):
            red_copy(r, k).wait_recv()
            total += red[r, (q + 8 - k) % 8].astype(jnp.float32)
        return total.astype(out.dtype)

    def fin_copy(r):
        to = plane_at(r)
        return remote(
            fin.at[r], out.at[:, at_piece(z, q)], fin_send.at[r], fin_recv.at[(n - r) % n], g, to
        )

    def fin_got(s):
        at = out.at[:, at_piece(plane_at(s), q)]
        return remote(fin.at[s], at, fin_send.at[s], fin_recv.at[s], g, plane_at(s))

    def finish(r):
        fin[r] = piece_sum(r)
        fin_copy(r).start()

    def out_plane(s, k):
        piece = out.at[:, at_piece(plane_at(s), q)]
        return remote(piece, piece, ob_send.at[s, k], ob_recv.at[s, k], chip_at(k), z)

    def out_plane_got(s, k):
        sender = (chip + 4 - k) % 4
        piece = out.at[:, at_piece(plane_at(s), core * 4 + sender)]
        return remote(piece, piece, ob_send.at[s, k], ob_recv.at[s, k], chip_at(k), z)

    def out_core(s):
        half = out.at[:, at_piece(plane_at(s), core * 4, 4)]
        return remote(half, half, oc_send.at[s], oc_recv.at[s], partner, z)

    def out_core_got(s):
        half = out.at[:, at_piece(plane_at(s), (1 - core) * 4, 4)]
        return remote(half, half, oc_send.at[s], oc_recv.at[s], partner, z)

    def spread(s):
        for k in range(1, 4):
            out_plane(s, k).start()

    def collect(s):
        for k in range(1, 4):
            out_plane_got(s, k).wait_recv()
        out_core(s).start()

    def act_plane_got(k):
        piece = act_all.at[pl.ds(1, n - 1), :, at_piece(0, core * 4 + (chip + 4 - k) % 4)]
        return remote(piece, piece, ab_send.at[k], ab_recv.at[k], chip_at(k), z)

    def act_core_got():
        half = act_all.at[pl.ds(1, n - 1), :, at_piece(0, (1 - core) * 4, 4)]
        return remote(half, half, ac_send, ac_recv, partner, z)

    def act_z_got(r):
        at = act_all.at[r, :, at_piece(0, q)]
        return remote(at, at, aa_send.at[r], aa_recv.at[r], g, plane_at(r))

    load_cot.wait()
    partial(0)

    for r in range(1, n):
        act_z_got(r).wait_recv()
    for k in range(1, 4):
        act_plane(k).start()

    lefts, rights = z, n - 1 - z
    both = jnp.minimum(lefts, rights)
    slots, forwards = [], []
    for k in range(1, n):
        paired = k <= 2 * both
        distance = jnp.where(paired, (k + 1) // 2, k - both)
        side = jnp.where(paired, 1 - 2 * (k % 2), jnp.where(lefts > rights, -1, 1))
        r = (side * distance + n) % n
        to = z - side
        inside = jnp.logical_and(to >= 0, to < n)
        forward = remote(
            cot_all.at[r], cot_all.at[(r + side + n) % n], cot_send.at[r],
            cot_recv.at[(r + side + n) % n], g, jnp.where(inside, to, z + side),
        )
        slots.append(r)
        forwards.append((inside, forward))
        remote(cot_all.at[r], cot_all.at[r], cot_send.at[r], cot_recv.at[r], g, z + side).wait_recv()

        @pl.when(inside)
        def _(forward=forward):
            forward.start()

        partial(r)
        if k == 1:
            out[:, at_piece(z, q)] = piece_sum(0)
            spread(0)
            for j in range(1, 4):
                act_plane_got(j).wait_recv()
            act_core().start()
        else:
            finish(slots[k - 2])
        if k >= 3:
            fin_got(slots[k - 3]).wait_recv()
            spread(slots[k - 3])

    load_act.wait()
    act_core_got().wait_recv()

    tokens = toks * n
    chunk = 384
    starts = list(range(0, hidden, chunk))

    def gq_copy(i):
        rows = pl.ds(starts[i], min(chunk, hidden - starts[i]))
        return pltpu.make_async_copy(gq_v.at[rows, :], gq.at[rows, :], gq_sem.at[i])

    def weight_grad(i):
        begin, size = starts[i], min(chunk, hidden - starts[i])
        lhs = cot_all[:, :, begin : begin + size].reshape(tokens, size)
        grad = lax.dot_general(
            lhs, act_all[...].reshape(tokens, cols), (((0,), (0,)), ((), ())),
            preferred_element_type=jnp.float32,
        ) * (1.0 / tokens)
        for j in range(cols // QCOLS):
            block = grad[:, j * QCOLS : (j + 1) * QCOLS].reshape(size // QROWS, QROWS, QCOLS)
            peak = jnp.max(jnp.max(jnp.abs(block), axis=1), axis=1, keepdims=True) + epsilon
            gscale[begin // QROWS : (begin + size) // QROWS, j : j + 1] = peak
            scaled = block * (1.0 / peak)[:, :, None]
            gq_v[begin : begin + size, j * QCOLS : (j + 1) * QCOLS] = scaled.reshape(size, QCOLS).astype(gq_v.dtype)
        gq_copy(i).start()

    weight_grad(0)
    finish(slots[n - 2])
    collect(0)
    fin_got(slots[n - 3]).wait_recv()
    spread(slots[n - 3])
    weight_grad(1)
    fin_got(slots[n - 2]).wait_recv()
    spread(slots[n - 2])
    for s in slots[:-1]:
        collect(s)
    for i in range(2, len(starts) - 1):
        weight_grad(i)
    collect(slots[n - 2])
    weight_grad(len(starts) - 1)

    out_core_got(0).wait_recv()
    for s in slots:
        out_core_got(s).wait_recv()

    @pl.when(z < n - 1)
    def _():
        own_right.wait_send()

    @pl.when(z > 0)
    def _():
        own_left.wait_send()

    for inside, forward in forwards:
        @pl.when(inside)
        def _(forward=forward):
            forward.wait_send()

    for r in range(1, n):
        act_z(r).wait_send()
        fin_copy(r).wait_send()
    for k in range(1, 4):
        act_plane(k).wait_send()
    act_core().wait_send()
    for r in range(n):
        for k in range(1, 8):
            red_copy(r, k).wait_send()
        for k in range(1, 4):
            out_plane(r, k).wait_send()
        out_core(r).wait_send()
    for i in range(len(starts)):
        gq_copy(i).wait()


def per_device(activations, cotangent, weight_quant, weight_scale):
    n = lax.axis_size("intra")
    toks, width = activations.shape
    hidden, cols = weight_quant.shape
    scale_rows = jnp.repeat(weight_scale, QROWS, axis=0)
    bf16, dma, vmem = jnp.bfloat16, pltpu.SemaphoreType.DMA, pltpu.VMEM
    hbm = pl.BlockSpec(memory_space=pl.ANY)
    inside = pl.BlockSpec(memory_space=pltpu.VMEM)
    return pl.pallas_call(
        functools.partial(kernel, n),
        out_shape=(
            jax.ShapeDtypeStruct((toks, width), bf16),
            jax.ShapeDtypeStruct((hidden, cols), bf16),
            jax.ShapeDtypeStruct((hidden // QROWS, cols // QCOLS), jnp.float32),
        ),
        in_specs=[hbm, hbm, hbm, inside],
        out_specs=(inside, hbm, inside),
        scratch_shapes=[
            vmem((n, toks, hidden), bf16),
            vmem((n, toks, cols), bf16),
            vmem((hidden, cols), bf16),
            vmem((hidden, cols), bf16),
            vmem((n, toks, cols), bf16),
            vmem((n, 8, toks, cols // 8), bf16),
            vmem((n, toks, cols // 8), bf16),
            vmem((hidden, cols), bf16),
            dma((3,)),
            dma((n + 1,)), dma((n,)),
            dma((n,)), dma((n,)),
            dma((4,)), dma((4,)),
            dma, dma,
            dma((n, 8)), dma((n, 8)),
            dma((n,)), dma((n,)),
            dma((n, 4)), dma((n, 4)),
            dma((n,)), dma((n,)),
            dma((pl.cdiv(hidden, 384),)),
        ],
        compiler_params=pltpu.CompilerParams(
            collective_id=0, has_side_effects=True, vmem_limit_bytes=56 * 1024 * 1024
        ),
        cost_estimate=pl.CostEstimate(
            flops=4 * n * toks * hidden * cols, bytes_accessed=4 * hidden * cols, transcendentals=0
        ),
    )(activations, cotangent, weight_quant, scale_rows)


def solution(mesh):
    planes = mesh.shape["grp"] == 8 and mesh.shape["intra"] == 4
    return jax.shard_map(
        per_device if planes else general,
        mesh=mesh,
        in_specs=(P("intra", None), P("intra", "grp"), P("grp", "intra"), P("grp", "intra")),
        out_specs=(P("intra", None), P("grp", "intra"), P("grp", "intra")),
        check_vma=False,
    )
```

```python
import functools

import jax
import jax.numpy as jnp
from jax import lax
from jax.experimental import pallas as pl
from jax.experimental.pallas import tpu as pltpu
from jax.sharding import PartitionSpec as P

QROWS = 8
QCOLS = 256
MESH = pl.DeviceIdType.MESH

epsilon = 1e-06


def dequantize(quantized, scales):
    row_count, col_count = quantized.shape
    blocks = quantized.astype(jnp.float32).reshape(
        row_count // QROWS, QROWS, col_count // QCOLS, QCOLS
    )
    return (blocks * scales.astype(jnp.float32)[:, None, :, None]).reshape(row_count, col_count)


def summed_rows(source, weight):
    shares = lax.psum_scatter(
        jnp.dot(source, weight, preferred_element_type=jnp.float32),
        "grp",
        scatter_dimension=0,
        tiled=True,
    )
    return lax.all_gather(shares.astype(jnp.bfloat16), "grp", axis=0, tiled=True)


def requantize(summed):
    block_count, _, local_cols = summed.shape
    blocks = summed.reshape(block_count, QROWS, local_cols // QCOLS, QCOLS)
    peak_value = jnp.max(jnp.abs(blocks), axis=(1, 3)) + epsilon
    requant = (blocks / peak_value[:, None, :, None]).astype(jnp.bfloat16)
    return (requant.reshape(block_count, QROWS, local_cols), peak_value)


def general(activations, cotangent, weight_quant, weight_scale):
    intra_count = lax.axis_size("intra")
    quant_all, scale_all = (
        lax.all_gather(weight_quant, "intra", axis=1, tiled=True),
        lax.all_gather(weight_scale, "intra", axis=1, tiled=True),
    )
    weight = dequantize(quant_all, scale_all).astype(jnp.bfloat16)
    total_tokens = activations.shape[0] * intra_count
    tok_rows = activations.shape[0]
    hidden_rows = cotangent.shape[1]
    act_cols = lax.all_to_all(activations, "intra", split_axis=1, concat_axis=0, tiled=True)
    cot_all = lax.all_gather(cotangent, "intra", axis=0, tiled=True)
    input_grad = summed_rows(cotangent, weight)
    local_cols = act_cols.shape[1]
    act_split = act_cols.reshape(intra_count, tok_rows, local_cols)
    cot_split = cot_all.reshape(intra_count, tok_rows, hidden_rows)
    partials = (
        jnp.einsum("bth,btc->bhc", cot_split, act_split, preferred_element_type=jnp.float32)
        / total_tokens
    )
    partials = lax.optimization_barrier(partials.astype(jnp.bfloat16))
    summed = jnp.sum(partials.astype(jnp.float32), axis=0)
    grad_quant, grad_scale = requantize(summed.reshape(hidden_rows // QROWS, QROWS, local_cols))
    grad_quant = grad_quant.reshape(hidden_rows, local_cols)
    return (input_grad, grad_quant, grad_scale)


def kernel(
    n, act, cot, wq, wscale, out, gq, gscale,
    cot_all, act_all, wq_v, w, psend, red, fin, gq_v, scale_v, peaks,
    local_sem, cot_send, cot_recv, aa_send, aa_recv, ab_send, ab_recv, ac_send, ac_recv,
    red_send, red_recv, fin_send, fin_recv, ob_send, ob_recv, oc_send, oc_recv, gq_sem,
):
    g, z = lax.axis_index("grp"), lax.axis_index("intra")
    chip, core = g // 2, g % 2
    q = core * 4 + chip
    toks = cot.shape[0]
    hidden, cols = wq.shape
    width = cols // 8
    partner = chip * 2 + (1 - core)

    def at_piece(plane, piece, count=1):
        return pl.ds(pl.multiple_of(plane * cols + piece * width, width), count * width)

    def chip_at(k):
        return ((chip + k) % 4) * 2 + core

    def plane_at(r):
        return (z + r) % n

    def remote(src, dst, send, recv, to_g, to_z):
        return pltpu.make_async_remote_copy(
            src_ref=src, dst_ref=dst, send_sem=send, recv_sem=recv,
            device_id=(to_g, to_z), device_id_type=MESH,
        )

    load_wq = pltpu.make_async_copy(wq, wq_v, local_sem.at[0])
    load_cot = pltpu.make_async_copy(cot, cot_all.at[0], local_sem.at[1])
    load_act = pltpu.make_async_copy(
        act.at[:, pl.ds(pl.multiple_of(z * cols, width), cols)], act_all.at[0], local_sem.at[2]
    )
    load_cot.start()
    load_wq.start()
    load_act.start()

    barrier = pltpu.get_barrier_semaphore()
    for k in range(1, 8):
        t = (q + k) % 8
        pl.semaphore_signal(barrier, inc=1, device_id=((t % 4) * 2 + t // 4, z), device_id_type=MESH)
    for r in range(1, n):
        pl.semaphore_signal(barrier, inc=1, device_id=(g, plane_at(r)), device_id_type=MESH)
    pl.semaphore_wait(barrier, 7 + n - 1)

    own_right = remote(cot, cot_all.at[n - 1], cot_send.at[n], cot_recv.at[n - 1], g, jnp.minimum(z + 1, n - 1))
    own_left = remote(cot, cot_all.at[1], cot_send.at[0], cot_recv.at[1], g, jnp.maximum(z - 1, 0))

    @pl.when(z < n - 1)
    def _():
        own_right.start()

    @pl.when(z > 0)
    def _():
        own_left.start()

    def act_z(r):
        to = plane_at(r)
        return remote(
            act.at[:, at_piece(to, q)], act_all.at[n - r, :, at_piece(0, q)],
            aa_send.at[r], aa_recv.at[n - r], g, to,
        )

    for r in range(1, n):
        act_z(r).start()

    def act_plane(k):
        piece = act_all.at[pl.ds(1, n - 1), :, at_piece(0, q)]
        return remote(piece, piece, ab_send.at[k], ab_recv.at[k], chip_at(k), z)

    def act_core():
        half = act_all.at[pl.ds(1, n - 1), :, at_piece(0, core * 4, 4)]
        return remote(half, half, ac_send, ac_recv, partner, z)

    scale_v[...] = wscale[...].astype(jnp.float32).T
    load_wq.wait()
    step = 480 if hidden % 480 == 0 else hidden

    @pl.loop(0, hidden // step)
    def _(i):
        rows = pl.ds(pl.multiple_of(i * step, step), step)
        scale = scale_v[pl.ds(i * (step // QROWS), step // QROWS), :]
        for j in range(cols // QCOLS):
            at = pl.ds(j * QCOLS, QCOLS)
            block = wq_v[rows, at].astype(jnp.float32).reshape(step // QROWS, QROWS, QCOLS)
            block = block * scale[:, j : j + 1][:, :, None]
            w[rows, at] = block.reshape(step, QCOLS).astype(w.dtype)

    def red_copy(r, k):
        t = (q + k) % 8
        return remote(
            psend.at[r, :, at_piece(0, t)], red.at[r, q],
            red_send.at[r, k], red_recv.at[r, k], (t % 4) * 2 + t // 4, z,
        )

    def partial(r):
        psend[r] = jnp.dot(cot_all[r], w[...], preferred_element_type=jnp.float32).astype(psend.dtype)
        for k in range(1, 8):
            red_copy(r, k).start()

    def piece_sum(r):
        total = psend[r, :, at_piece(0, q)].astype(jnp.float32)
        for k in range(1, 8):
            red_copy(r, k).wait_recv()
            total += red[r, (q + 8 - k) % 8].astype(jnp.float32)
        return total.astype(out.dtype)

    def fin_copy(r):
        to = plane_at(r)
        return remote(
            fin.at[r], out.at[:, at_piece(z, q)], fin_send.at[r], fin_recv.at[(n - r) % n], g, to
        )

    def fin_got(s):
        at = out.at[:, at_piece(plane_at(s), q)]
        return remote(fin.at[s], at, fin_send.at[s], fin_recv.at[s], g, plane_at(s))

    def finish(r):
        fin[r] = piece_sum(r)
        fin_copy(r).start()

    def out_plane(s, k):
        piece = out.at[:, at_piece(plane_at(s), q)]
        return remote(piece, piece, ob_send.at[s, k], ob_recv.at[s, k], chip_at(k), z)

    def out_plane_got(s, k):
        sender = (chip + 4 - k) % 4
        piece = out.at[:, at_piece(plane_at(s), core * 4 + sender)]
        return remote(piece, piece, ob_send.at[s, k], ob_recv.at[s, k], chip_at(k), z)

    def out_core(s):
        half = out.at[:, at_piece(plane_at(s), core * 4, 4)]
        return remote(half, half, oc_send.at[s], oc_recv.at[s], partner, z)

    def out_core_got(s):
        half = out.at[:, at_piece(plane_at(s), (1 - core) * 4, 4)]
        return remote(half, half, oc_send.at[s], oc_recv.at[s], partner, z)

    def spread(s):
        for k in range(1, 4):
            out_plane(s, k).start()

    def collect(s):
        for k in range(1, 4):
            out_plane_got(s, k).wait_recv()
        out_core(s).start()

    def act_plane_got(k):
        piece = act_all.at[pl.ds(1, n - 1), :, at_piece(0, core * 4 + (chip + 4 - k) % 4)]
        return remote(piece, piece, ab_send.at[k], ab_recv.at[k], chip_at(k), z)

    def act_core_got():
        half = act_all.at[pl.ds(1, n - 1), :, at_piece(0, (1 - core) * 4, 4)]
        return remote(half, half, ac_send, ac_recv, partner, z)

    def act_z_got(r):
        at = act_all.at[r, :, at_piece(0, q)]
        return remote(at, at, aa_send.at[r], aa_recv.at[r], g, plane_at(r))

    lefts, rights = z, n - 1 - z
    both = jnp.minimum(lefts, rights)
    slots, forwards, arrive = [], [], []
    for k in range(1, n):
        paired = k <= 2 * both
        distance = jnp.where(paired, (k + 1) // 2, k - both)
        side = jnp.where(paired, 1 - 2 * (k % 2), jnp.where(lefts > rights, -1, 1))
        r = (side * distance + n) % n
        to = z - side
        inside = jnp.logical_and(to >= 0, to < n)
        forward = remote(
            cot_all.at[r], cot_all.at[(r + side + n) % n], cot_send.at[r],
            cot_recv.at[(r + side + n) % n], g, jnp.where(inside, to, z + side),
        )
        got = remote(cot_all.at[r], cot_all.at[r], cot_send.at[r], cot_recv.at[r], g, z + side)
        slots.append(r)
        forwards.append((inside, forward))

        def land(got=got, inside=inside, forward=forward):
            got.wait_recv()

            @pl.when(inside)
            def _():
                forward.start()

        arrive.append(land)

    load_cot.wait()
    partial(0)

    for k in range(1, n):
        if k % 2 == 1:
            arrive[k - 1]()
            if k + 1 < n:
                pl.when(k + 1 <= 2 * both)(arrive[k])
        else:
            pl.when(k > 2 * both)(arrive[k - 1])
        partial(slots[k - 1])
        if k == 1:
            for r in range(1, n):
                act_z_got(r).wait_recv()
            for j in range(1, 4):
                act_plane(j).start()
            out[:, at_piece(z, q)] = piece_sum(0)
            spread(0)
        else:
            finish(slots[k - 2])
        if k >= 3:
            fin_got(slots[k - 3]).wait_recv()
            spread(slots[k - 3])
            if k == 3:
                for j in range(1, 4):
                    act_plane_got(j).wait_recv()
                act_core().start()

    load_act.wait()
    act_core_got().wait_recv()

    tokens = toks * n
    chunk = 384
    starts = list(range(0, hidden, chunk))

    def gq_copy(i):
        rows = pl.ds(starts[i], min(chunk, hidden - starts[i]))
        return pltpu.make_async_copy(gq_v.at[rows, :], gq.at[rows, :], gq_sem.at[i])

    def weight_grad(i):
        begin, size = starts[i], min(chunk, hidden - starts[i])
        lhs = cot_all[:, :, begin : begin + size].reshape(tokens, size)
        grad = lax.dot_general(
            lhs, act_all[...].reshape(tokens, cols), (((0,), (0,)), ((), ())),
            preferred_element_type=jnp.float32,
        ) * (1.0 / tokens)
        for j in range(cols // QCOLS):
            block = grad[:, j * QCOLS : (j + 1) * QCOLS].reshape(size // QROWS, QROWS, QCOLS)
            peak = jnp.max(jnp.max(jnp.abs(block), axis=1), axis=1, keepdims=True) + epsilon
            peaks[begin // QROWS : (begin + size) // QROWS, j : j + 1] = peak
            scaled = block * (1.0 / peak)[:, :, None]
            gq_v[begin : begin + size, j * QCOLS : (j + 1) * QCOLS] = scaled.reshape(size, QCOLS).astype(gq_v.dtype)
        gq_copy(i).start()

    weight_grad(0)
    finish(slots[n - 2])
    weight_grad(1)
    fin_got(slots[n - 3]).wait_recv()
    spread(slots[n - 3])
    collect(0)
    fin_got(slots[n - 2]).wait_recv()
    spread(slots[n - 2])
    weight_grad(2)
    for s in slots[:-1]:
        collect(s)
    collect(slots[n - 2])
    for i in range(3, len(starts)):
        weight_grad(i)
    gscale[...] = peaks[...].T

    out_core_got(0).wait_recv()
    for s in slots:
        out_core_got(s).wait_recv()

    @pl.when(z < n - 1)
    def _():
        own_right.wait_send()

    @pl.when(z > 0)
    def _():
        own_left.wait_send()

    for inside, forward in forwards:
        @pl.when(inside)
        def _(forward=forward):
            forward.wait_send()

    for r in range(1, n):
        act_z(r).wait_send()
        fin_copy(r).wait_send()
    for k in range(1, 4):
        act_plane(k).wait_send()
    act_core().wait_send()
    for r in range(n):
        for k in range(1, 8):
            red_copy(r, k).wait_send()
        for k in range(1, 4):
            out_plane(r, k).wait_send()
        out_core(r).wait_send()
    for i in range(len(starts)):
        gq_copy(i).wait()


def per_device(activations, cotangent, weight_quant, weight_scale):
    n = lax.axis_size("intra")
    toks, width = activations.shape
    hidden, cols = weight_quant.shape
    bf16, dma, vmem = jnp.bfloat16, pltpu.SemaphoreType.DMA, pltpu.VMEM
    hbm = pl.BlockSpec(memory_space=pl.ANY)
    inside = pl.BlockSpec(memory_space=pltpu.VMEM)
    input_grad, grad_quant, grad_scale = pl.pallas_call(
        functools.partial(kernel, n),
        out_shape=(
            jax.ShapeDtypeStruct((toks, width), bf16),
            jax.ShapeDtypeStruct((hidden, cols), bf16),
            jax.ShapeDtypeStruct((cols // QCOLS, hidden // QROWS), jnp.float32),
        ),
        in_specs=[pl.BlockSpec(memory_space=pltpu.HBM)] * 3 + [inside],
        out_specs=(inside, hbm, inside),
        scratch_shapes=[
            vmem((n, toks, hidden), bf16),
            vmem((n, toks, cols), bf16),
            vmem((hidden, cols), bf16),
            vmem((hidden, cols), bf16),
            vmem((n, toks, cols), bf16),
            vmem((n, 8, toks, cols // 8), bf16),
            vmem((n, toks, cols // 8), bf16),
            vmem((hidden, cols), bf16),
            vmem((hidden // QROWS, cols // QCOLS), jnp.float32),
            vmem((hidden // QROWS, cols // QCOLS), jnp.float32),
            dma((3,)),
            dma((n + 1,)), dma((n,)),
            dma((n,)), dma((n,)),
            dma((4,)), dma((4,)),
            dma, dma,
            dma((n, 8)), dma((n, 8)),
            dma((n,)), dma((n,)),
            dma((n, 4)), dma((n, 4)),
            dma((n,)), dma((n,)),
            dma((pl.cdiv(hidden, 384),)),
        ],
        compiler_params=pltpu.CompilerParams(
            collective_id=0, has_side_effects=True, vmem_limit_bytes=28 * 1024 * 1024
        ),
        cost_estimate=pl.CostEstimate(
            flops=4 * n * toks * hidden * cols, bytes_accessed=4 * hidden * cols, transcendentals=0
        ),
    )(activations, cotangent, weight_quant, weight_scale.T)
    return input_grad, grad_quant, grad_scale.T


def solution(mesh):
    planes = mesh.shape["grp"] == 8 and mesh.shape["intra"] == 4
    return jax.shard_map(
        per_device if planes else general,
        mesh=mesh,
        in_specs=(P("intra", None), P("intra", "grp"), P("grp", "intra"), P("grp", "intra")),
        out_specs=(P("intra", None), P("grp", "intra"), P("grp", "intra")),
        check_vma=False,
    )
```
